256 devices in a mesh: dp: 16 (over z, core), tensor: 16 (over y, x).
Axes of the slice: x: 4, y: 4, z: 8, core: 2. Of those that a mesh axis runs over, the one named last changes fastest.
Arguments:
- inputs: bfloat16 [16384, 12288], P(('dp', 'tensor')), may hold values from -6 to 6
- grad_out: bfloat16 [16384, 12288], P(('dp', 'tensor')), may hold values from -6 to 6
- gate_pre: bfloat16 [16384, 14336], P('dp', 'tensor'), may hold values from -8 to 8
- up_pre: bfloat16 [16384, 14336], P('dp', 'tensor'), may hold values from -6 to 6
- hidden_base: bfloat16 [16384, 14336], P('dp', 'tensor'), may hold values from -6 to 6
- block_tenant: int32 [512], P('dp'), may hold values from 0 to 31
- reduce_gate: bfloat16 [32, 12288, 32], P('dp', 'tensor'), may hold values from -0.0546875 to 0.0546875
- expand_gate: bfloat16 [32, 32, 14336], P('dp', None, 'tensor'), may hold values from -1 to 1
- reduce_up: bfloat16 [32, 12288, 32], P('dp', 'tensor'), may hold values from -0.0546875 to 0.0546875
- expand_up: bfloat16 [32, 32, 14336], P('dp', None, 'tensor'), may hold values from -1 to 1
- reduce_down: bfloat16 [32, 14336, 32], P('dp', 'tensor'), may hold values from -1 to 1
- expand_down: bfloat16 [32, 32, 12288], P('dp', None, 'tensor'), may hold values from -0.0546875 to 0.0546875
Outputs:
- input_grad: bfloat16 [16384, 12288], P(('dp', 'tensor'))
- grad_reduce_gate: bfloat16 [32, 12288, 32], P('dp', 'tensor')
- grad_expand_gate: bfloat16 [32, 32, 14336], P('dp', None, 'tensor')
- grad_reduce_up: bfloat16 [32, 12288, 32], P('dp', 'tensor')
- grad_expand_up: bfloat16 [32, 32, 14336], P('dp', None, 'tensor')
- grad_reduce_down: bfloat16 [32, 14336, 32], P('dp', 'tensor')
- grad_expand_down: bfloat16 [32, 32, 12288], P('dp', None, 'tensor')
The draws below stay inside these ranges and needn't reach their ends.
All inputs are finite; a program needn't handle non-finite values.
Results may differ from the reference program's by a relative error of at most 0.035.
Values may be sent and summed in bfloat16 or wider, within the bound.
No kernel may reach another device: no remote copies, remote signals or barrier semaphores. Data moves between devices by JAX's collectives and lax.ppermute only.
A program may use at most 128 MiB of HBM per device.

```python
import math
import jax
import jax.numpy as jnp
import numpy as np
from jax import lax

D = 12288
FF = 14336
TENANTS = 32
RANK = 32
BLOCK_ROWS = 32
GROUP_ROWS = 1024
TOKENS = 16384
BLOCKS = 512
N_DP = 16


def place_ends(values, rng, smallest, top_value):
    longest = values.shape.index(max(values.shape))
    spots = []
    for shift in (0, 1):
        where = [jax.random.randint(jax.random.fold_in(rng, axis), (), 0, length) for axis, length in enumerate(values.shape)]
        where[longest] = (where[longest] + shift) % values.shape[longest]
        spots.append(tuple(where))
    return values.at[spots[0]].set(smallest).at[spots[1]].set(top_value)


def shard_levels(stream_key, dims, pieces, low, high):
    def one(position, blocks):
        steps = jax.random.uniform(jax.random.fold_in(jax.random.fold_in(stream_key, 6), position), (blocks,), jnp.float32, low / len(pieces), high / len(pieces))
        return jnp.repeat(jnp.exp(steps), dims[position] // blocks).reshape((-1,) + (1,) * (len(dims) - position - 1))

    level = one(*pieces[0])
    for cut in pieces[1:]:
        level = level * one(*cut)
    return level


def rank_bounds(number_of, skew):
    portions = [(1 << 20) // math.isqrt(standing ** skew) + 1 for standing in range(1, number_of + 1)]
    scale = 1 + sum(portions) // (1 << 30)
    return np.cumsum(np.array([max(1, weight // scale) for weight in portions]))


def ranked_ids(stream_key, shape, count, skew):
    grid = rank_bounds(count, skew)
    ticket = jax.random.randint(jax.random.fold_in(stream_key, 1), shape, 0, int(grid[count - 1]))
    rank = jnp.searchsorted(jnp.asarray(grid, jnp.int32), ticket, side="right")
    return jax.random.permutation(jax.random.fold_in(stream_key, 2), count)[rank].astype(jnp.int32)


def normal_values(key, extent, spread, bound, shards=(), kind=jnp.bfloat16):
    factor_of = shard_levels(key, extent, shards, -0.22, 0.18) if shards else 1.0
    result = jax.random.normal(key, extent, jnp.float32) * spread * factor_of
    return jnp.minimum(jnp.maximum(result, -bound), bound).astype(kind)


def setup_inputs(seed: int = 0) -> dict:
    key_of = jax.random.split(jax.random.key(seed), 13)
    return {
        "inputs": normal_values(key_of[0], (TOKENS, D), 1.0, 6.0, ((0, 256),)),
        "grad_out": normal_values(key_of[1], (TOKENS, D), 1.0, 6.0, ((0, 256),)),
        "gate_pre": normal_values(key_of[2], (TOKENS, FF), 1.5, 8.0, ((0, 16), (1, 16))),
        "up_pre": normal_values(key_of[3], (TOKENS, FF), 1.0, 6.0, ((0, 16), (1, 16))),
        "hidden_base": normal_values(key_of[4], (TOKENS, FF), 1.0, 6.0, ((0, 16), (1, 16))),
        "block_tenant": place_ends(ranked_ids(key_of[5], (BLOCKS,), TENANTS, 2), jax.random.fold_in(key_of[5], 3), 0, TENANTS - 1).astype(jnp.int32),
        "reduce_gate": normal_values(key_of[6], (TENANTS, D, RANK), D ** -0.5, 0.0546875, ((0, 16), (1, 16))),
        "expand_gate": normal_values(key_of[7], (TENANTS, RANK, FF), RANK ** -0.5, 1.0, ((0, 16), (2, 16))),
        "reduce_up": normal_values(key_of[8], (TENANTS, D, RANK), D ** -0.5, 0.0546875, ((0, 16), (1, 16))),
        "expand_up": normal_values(key_of[9], (TENANTS, RANK, FF), RANK ** -0.5, 1.0, ((0, 16), (2, 16))),
        "reduce_down": normal_values(key_of[10], (TENANTS, FF, RANK), RANK ** -0.5, 1.0, ((0, 16), (1, 16))),
        "expand_down": normal_values(key_of[11], (TENANTS, RANK, D), D ** -0.5, 0.0546875, ((0, 16), (2, 16))),
    }


def tenant_sum(onehot, blocks):
    return jnp.einsum('bt,bxy->txy', onehot, blocks)


def reference(inputs, grad_out, gate_pre, up_pre, hidden_base, block_tenant, reduce_gate, expand_gate, reduce_up, expand_up, reduce_down, expand_down):
    fdt = jnp.float32
    block_count = GROUP_ROWS // BLOCK_ROWS
    items = (inputs.reshape(N_DP, GROUP_ROWS, D), grad_out.reshape(N_DP, GROUP_ROWS, D),
             gate_pre.reshape(N_DP, GROUP_ROWS, FF), up_pre.reshape(N_DP, GROUP_ROWS, FF),
             hidden_base.reshape(N_DP, GROUP_ROWS, FF), block_tenant.reshape(N_DP, block_count))

    def group_pass(carry, item):
        inp, outg, gate, upv, hbase, tenant = item
        pick_rg = jnp.take(reduce_gate, tenant, axis=0).astype(fdt)
        pick_eg = jnp.take(expand_gate, tenant, axis=0).astype(fdt)
        pick_ru = jnp.take(reduce_up, tenant, axis=0).astype(fdt)
        pick_eu = jnp.take(expand_up, tenant, axis=0).astype(fdt)
        pick_rd = jnp.take(reduce_down, tenant, axis=0).astype(fdt)
        pick_ed = jnp.take(expand_down, tenant, axis=0).astype(fdt)
        inpb = inp.reshape(block_count, BLOCK_ROWS, D).astype(fdt)
        outb = outg.reshape(block_count, BLOCK_ROWS, D).astype(fdt)
        gatef = gate.reshape(block_count, BLOCK_ROWS, FF).astype(fdt)
        upf = upv.reshape(block_count, BLOCK_ROWS, FF).astype(fdt)
        basef = hbase.reshape(block_count, BLOCK_ROWS, FF).astype(fdt)
        gate_low = jnp.einsum('bnd,bdr->bnr', inpb, pick_rg).astype(jnp.bfloat16)
        up_low = jnp.einsum('bnd,bdr->bnr', inpb, pick_ru).astype(jnp.bfloat16)
        grad_low = jnp.einsum('bnd,brd->bnr', outb, pick_ed).astype(jnp.bfloat16)
        sig = jax.nn.sigmoid(gatef)
        silu = gatef * sig
        slope = sig * (1.0 + gatef * (1.0 - sig))
        hidden = (silu * upf).astype(jnp.bfloat16)
        down_low = jnp.einsum('bnf,bfr->bnr', hidden.astype(fdt), pick_rd).astype(jnp.bfloat16)
        hidden_grad = basef + jnp.einsum('bnr,bfr->bnf', grad_low.astype(fdt), pick_rd)
        gate_grad = (hidden_grad * upf * slope).astype(jnp.bfloat16)
        up_grad = (hidden_grad * silu).astype(jnp.bfloat16)
        gate_back = jnp.einsum('bnf,brf->bnr', gate_grad.astype(fdt), pick_eg).astype(jnp.bfloat16)
        up_back = jnp.einsum('bnf,brf->bnr', up_grad.astype(fdt), pick_eu).astype(jnp.bfloat16)
        dx_rows = jnp.einsum('bnr,bdr->bnd', gate_back.astype(fdt), pick_rg) + jnp.einsum('bnr,bdr->bnd', up_back.astype(fdt), pick_ru)
        dx_rows = dx_rows.astype(jnp.bfloat16).reshape(GROUP_ROWS, D)
        onehot = (tenant[:, None] == jnp.arange(TENANTS, dtype=jnp.int32)[None, :]).astype(fdt)
        parts = (
            tenant_sum(onehot, jnp.einsum('bnd,bnr->bdr', inpb, gate_back.astype(fdt))),
            tenant_sum(onehot, jnp.einsum('bnr,bnf->brf', gate_low.astype(fdt), gate_grad.astype(fdt))),
            tenant_sum(onehot, jnp.einsum('bnd,bnr->bdr', inpb, up_back.astype(fdt))),
            tenant_sum(onehot, jnp.einsum('bnr,bnf->brf', up_low.astype(fdt), up_grad.astype(fdt))),
            tenant_sum(onehot, jnp.einsum('bnf,bnr->bfr', hidden.astype(fdt), grad_low.astype(fdt))),
            tenant_sum(onehot, jnp.einsum('bnr,bnd->brd', down_low.astype(fdt), outb)),
        )
        new_carry = tuple(c + p.astype(jnp.bfloat16).astype(fdt) for c, p in zip(carry, parts))
        return new_carry, dx_rows

    start = (jnp.zeros((TENANTS, D, RANK), fdt), jnp.zeros((TENANTS, RANK, FF), fdt),
             jnp.zeros((TENANTS, D, RANK), fdt), jnp.zeros((TENANTS, RANK, FF), fdt),
             jnp.zeros((TENANTS, FF, RANK), fdt), jnp.zeros((TENANTS, RANK, D), fdt))
    sums, dx_all = lax.scan(group_pass, start, items)
    input_grad = dx_all.reshape(TOKENS, D)
    return (input_grad, sums[0].astype(jnp.bfloat16), sums[1].astype(jnp.bfloat16),
            sums[2].astype(jnp.bfloat16), sums[3].astype(jnp.bfloat16),
            sums[4].astype(jnp.bfloat16), sums[5].astype(jnp.bfloat16))
```

```python
import jax
import jax.numpy as jnp
from jax import lax
from jax.sharding import PartitionSpec as P

BF = jnp.bfloat16
F32 = jnp.float32
SIDE = 4


def shift(value, axis_of, step):
    pairs = []
    for y in range(SIDE):
        for x in range(SIDE):
            ny, nx = (y, (x + step) % SIDE) if axis_of == "x" else ((y + step) % SIDE, x)
            pairs.append((y * SIDE + x, ny * SIDE + nx))
    return lax.ppermute(value, "tensor", pairs)


def side_sum(value, axis_of):
    others = [shift(value, axis_of, step) for step in (1, 3, 2)]
    total = value.astype(F32)
    for other in others:
        total = total + other.astype(F32)
    return total.astype(BF)


def plane_sum(value):
    return side_sum(side_sum(value, "x"), "y")


def mm(left, right, dims):
    return lax.dot_general(left, right, (dims, ((), ())), preferred_element_type=F32)


def local(
    inputs,
    grad_out,
    gate_pre,
    up_pre,
    hidden_base,
    block_tenant,
    reduce_gate,
    expand_gate,
    reduce_up,
    expand_up,
    reduce_down,
    expand_down,
):
    n_dp = lax.axis_size("dp")
    own, rank, ff = expand_gate.shape
    d = expand_down.shape[2]
    m = own * n_dp * rank
    blocks = block_tenant.shape[0]
    n = gate_pre.shape[0]
    flip = lambda t: jnp.swapaxes(t, 1, 2)
    packed = jnp.concatenate(
        [expand_down, flip(reduce_gate), flip(reduce_up), flip(reduce_down), expand_gate, expand_up],
        axis=2,
    ).reshape(own * rank, 3 * d + 3 * ff)
    table = lax.all_gather(packed, "dp", axis=0, tiled=True)
    ed, rg, ru = table[:, :d], table[:, d : 2 * d], table[:, 2 * d : 3 * d]
    rd, eg, eu = (
        table[:, 3 * d : 3 * d + ff],
        table[:, 3 * d + ff : 3 * d + 2 * ff],
        table[:, 3 * d + 2 * ff :],
    )
    outg = lax.all_to_all(grad_out, "tensor", split_axis=1, concat_axis=0, tiled=True)
    inp = lax.all_to_all(inputs, "tensor", split_axis=1, concat_axis=0, tiled=True)

    row_tenant = jnp.repeat(block_tenant, n // blocks)
    column = lax.broadcasted_iota(jnp.int32, (n, m), 1) // rank
    mask = row_tenant[:, None] == column
    spread = (
        lax.broadcasted_iota(jnp.int32, (m, rank), 0) % rank
        == lax.broadcasted_iota(jnp.int32, (m, rank), 1)
    ).astype(BF)

    def low(rows, factors):
        dense = mm(rows, factors, ((1,), (1,)))
        picked = jnp.where(mask, dense, 0.0).astype(BF)
        return mm(spread, picked, ((0,), (1,))).astype(BF)

    def widen(low_t):
        wide = mm(low_t, spread, ((0,), (1,)))
        return jnp.where(mask, wide, 0.0).astype(BF)

    gate = gate_pre.astype(F32)
    up = up_pre.astype(F32)
    sig = jax.nn.sigmoid(gate)
    silu = gate * sig
    slope = sig * (1.0 + gate * (1.0 - sig))
    hidden = (silu * up).astype(BF)

    grad_low = plane_sum(low(outg, ed))
    gate_low, up_low, down_low = jnp.split(
        plane_sum(jnp.concatenate([low(inp, rg), low(inp, ru), low(hidden, rd)])), 3
    )
    grad_wide = widen(grad_low)
    hidden_grad = hidden_base.astype(F32) + mm(grad_wide, rd, ((1,), (0,)))
    gate_grad = (hidden_grad * up * slope).astype(BF)
    up_grad = (hidden_grad * silu).astype(BF)
    gate_back, up_back = jnp.split(
        plane_sum(jnp.concatenate([low(gate_grad, eg), low(up_grad, eu)])), 2
    )
    grad_rd = mm(grad_wide, hidden, ((0,), (0,))).astype(BF)
    grad_ed = mm(widen(down_low), outg, ((0,), (0,))).astype(BF)
    grad_eg = mm(widen(gate_low), gate_grad, ((0,), (0,))).astype(BF)
    grad_eu = mm(widen(up_low), up_grad, ((0,), (0,))).astype(BF)
    gate_wide, up_wide = widen(gate_back), widen(up_back)
    grad_rg = mm(gate_wide, inp, ((0,), (0,))).astype(BF)
    grad_ru = mm(up_wide, inp, ((0,), (0,))).astype(BF)
    dx = mm(gate_wide, rg, ((1,), (0,))) + mm(up_wide, ru, ((1,), (0,)))
    input_grad = lax.all_to_all(dx.astype(BF), "tensor", split_axis=0, concat_axis=1, tiled=True)
    grads = jnp.concatenate([grad_rg, grad_ru, grad_ed, grad_rd, grad_eg, grad_eu], axis=1)
    sums = lax.psum_scatter(grads, "dp", scatter_dimension=0, tiled=True)
    sums = sums.reshape(own, rank, 3 * d + 3 * ff)
    return (
        input_grad,
        flip(sums[:, :, :d]),
        sums[:, :, 3 * d + ff : 3 * d + 2 * ff],
        flip(sums[:, :, d : 2 * d]),
        sums[:, :, 3 * d + 2 * ff :],
        flip(sums[:, :, 3 * d : 3 * d + ff]),
        sums[:, :, 2 * d : 3 * d],
    )


def solution(mesh):
    in_specs = (
        P(("dp", "tensor"), None),
        P(("dp", "tensor"), None),
        P("dp", "tensor"),
        P("dp", "tensor"),
        P("dp", "tensor"),
        P("dp"),
        P("dp", "tensor", None),
        P("dp", None, "tensor"),
        P("dp", "tensor", None),
        P("dp", None, "tensor"),
        P("dp", "tensor", None),
        P("dp", None, "tensor"),
    )
    out_specs = (
        P(("dp", "tensor"), None),
        P("dp", "tensor", None),
        P("dp", None, "tensor"),
        P("dp", "tensor", None),
        P("dp", None, "tensor"),
        P("dp", "tensor", None),
        P("dp", None, "tensor"),
    )
    return jax.shard_map(local, mesh=mesh, in_specs=in_specs, out_specs=out_specs, check_vma=False)
```

```python
import jax
import jax.numpy as jnp
from jax import lax
from jax.experimental import pallas as pl
from jax.experimental.pallas import tpu as pltpu
from jax.sharding import PartitionSpec as P

BF = jnp.bfloat16
F32 = jnp.float32
SIDE = 4
NT = (((1,), (1,)), ((), ()))
NN = (((1,), (0,)), ((), ()))
PARAMS = pltpu.CompilerParams(vmem_limit_bytes=56 * 1024 * 1024)


def shift(value, side, step):
    pairs = []
    for y in range(SIDE):
        for x in range(SIDE):
            to_y, to_x = (y, (x + step) % SIDE) if side == "x" else ((y + step) % SIDE, x)
            pairs.append((y * SIDE + x, to_y * SIDE + to_x))
    return lax.ppermute(value, "tensor", pairs)


def side_sum(value, side):
    total = value.astype(F32)
    for other in [shift(value, side, step) for step in (1, 3, 2)]:
        total = total + other.astype(F32)
    return total.astype(BF)


def plane_sum(value):
    return side_sum(side_sum(value, "x"), "y")


def dot(left, right, dims):
    return lax.dot_general(left, right, dims, preferred_element_type=F32)


def diagonal(size, rank):
    down = lax.broadcasted_iota(jnp.int32, (size, size), 0) // rank
    across = lax.broadcasted_iota(jnp.int32, (size, size), 1) // rank
    return down == across


def own_factors(tenant_ref, table_ref, held, rank):
    count = held.shape[0] // rank
    first = pl.program_id(0) * count
    for b in range(count):
        at = pl.multiple_of(tenant_ref[first + b] * rank, rank)
        held[b * rank : (b + 1) * rank, :] = table_ref[pl.ds(at, rank), :]


def pick(dense, rank):
    kept = jnp.where(diagonal(dense.shape[0], rank), dense, 0.0)
    return kept.reshape(-1, rank, kept.shape[1]).sum(axis=0).astype(BF)


def widen(low_t):
    rank, step = low_t.shape
    quad = jnp.concatenate([low_t.astype(F32)] * (128 // rank), axis=0).T
    wide = jnp.concatenate([quad] * (step // 128), axis=1)
    return jnp.where(diagonal(step, rank), wide, 0.0).astype(BF)


def widen_t(low_t, same):
    wide = jnp.concatenate([low_t.astype(F32)] * (same.shape[0] // low_t.shape[0]), axis=0)
    return jnp.where(same, wide, 0.0).astype(BF)


def table_spec(m, width, at):
    return pl.BlockSpec((pl.Element(m), pl.Element(width)), lambda i, k: (0, at))


def cost(flops, moved, exps=0):
    return pl.CostEstimate(flops=flops, bytes_accessed=moved, transcendentals=exps)


def pack(groups):
    own, rank, _ = groups[0][0].shape
    flat = [part for group in groups for part in group]

    def kernel(*refs):
        ins, outs = list(refs[: len(flat)]), refs[len(flat) :]
        for out, group in zip(outs, groups):
            at = 0
            for part in group:
                ref = ins.pop(0)
                for t in range(own):
                    out[t * rank : (t + 1) * rank, at : at + part.shape[2]] = ref[t]
                at += part.shape[2]

    shapes = [
        jax.ShapeDtypeStruct((own * rank, sum(part.shape[2] for part in group)), BF)
        for group in groups
    ]
    return pl.pallas_call(kernel, out_shape=shapes, compiler_params=PARAMS)(*flat)


def rows_spec(swapped, which, step):
    _, _, each, width = swapped.shape
    return pl.BlockSpec((step // each, 1, each, width), lambda i, k: (i, which, 0, 0))


def fixed_rows(swapped, which):
    peers, _, each, width = swapped.shape
    return pl.BlockSpec((peers, 1, each, width), lambda i: (0, which, 0, 0))


def flat(ref):
    return ref[...].reshape(-1, ref.shape[-1])


def call(kernel, tenants, grid, in_specs, out_specs, out_shape, held, estimate, operands):
    return pl.pallas_call(
        kernel,
        grid_spec=pltpu.PrefetchScalarGridSpec(
            num_scalar_prefetch=1,
            grid=(grid,),
            in_specs=in_specs,
            out_specs=out_specs,
            scratch_shapes=[pltpu.VMEM(shape, BF) for shape in held],
        ),
        out_shape=out_shape,
        compiler_params=PARAMS,
        cost_estimate=estimate,
    )(tenants, *operands)


def low_one(tenants, swapped, which, table, at, rank, step=256):
    peers, _, each, width = swapped.shape
    n = peers * each
    m = table.shape[0]

    def kernel(k_ref, a_ref, t_ref, o_ref, held):
        own_factors(k_ref, t_ref, held, rank)
        o_ref[...] = pick(dot(held[...], flat(a_ref), NT), rank)

    return call(
        kernel,
        tenants,
        n // step,
        [rows_spec(swapped, which, step), table_spec(m, width, at)],
        pl.BlockSpec((rank, step), lambda i, k: (0, i)),
        jax.ShapeDtypeStruct((rank, n), BF),
        [(step, width)],
        cost(2 * n * step * width, 2 * (n + m) * width),
        [swapped, table],
    )


def low_three(tenants, swapped, which, gate_pre, up_pre, table, at_rg, at_rd, rank, step=256):
    d = swapped.shape[3]
    n, ff = gate_pre.shape
    m = table.shape[0]

    def kernel(k_ref, x_ref, g_ref, u_ref, rgu_ref, rd_ref, o_ref, h_ref, held, held_rd):
        own_factors(k_ref, rgu_ref, held, rank)
        own_factors(k_ref, rd_ref, held_rd, rank)
        gate = g_ref[...].astype(F32)
        hidden = (gate * jax.nn.sigmoid(gate) * u_ref[...].astype(F32)).astype(BF)
        h_ref[...] = hidden
        rows = flat(x_ref)
        o_ref[:rank, :] = pick(dot(held[:, :d], rows, NT), rank)
        o_ref[rank : 2 * rank, :] = pick(dot(held[:, d:], rows, NT), rank)
        o_ref[2 * rank :, :] = pick(dot(held_rd[...], hidden, NT), rank)

    block = pl.BlockSpec((step, ff), lambda i, k: (i, 0))
    return call(
        kernel,
        tenants,
        n // step,
        [
            rows_spec(swapped, which, step),
            block,
            block,
            table_spec(m, 2 * d, at_rg),
            table_spec(m, ff, at_rd),
        ],
        (pl.BlockSpec((3 * rank, step), lambda i, k: (0, i)), block),
        (jax.ShapeDtypeStruct((3 * rank, n), BF), jax.ShapeDtypeStruct((n, ff), BF)),
        [(step, 2 * d), (step, ff)],
        cost(2 * n * step * (2 * d + ff), 2 * (n + 2 * m) * d + 2 * (3 * n + m) * ff, n * ff),
        [swapped, gate_pre, up_pre, table, table],
    )


def middle(tenants, grad_low, gate_pre, up_pre, base, table, at_rd, step=256):
    n, ff = gate_pre.shape
    rank = grad_low.shape[0]
    m = table.shape[0]

    def kernel(k_ref, l_ref, g_ref, u_ref, b_ref, rd_ref, gg_ref, ug_ref, held):
        own_factors(k_ref, rd_ref, held, rank)
        grad = b_ref[...].astype(F32) + dot(widen(l_ref[...]), held[...], NN)
        gate = g_ref[...].astype(F32)
        s = jax.nn.sigmoid(gate)
        slope = s * (1.0 + gate * (1.0 - s))
        gg_ref[...] = (grad * u_ref[...].astype(F32) * slope).astype(BF)
        ug_ref[...] = (grad * (gate * s)).astype(BF)

    block = pl.BlockSpec((step, ff), lambda i, k: (i, 0))
    low = pl.BlockSpec((rank, step), lambda i, k: (0, i))
    return call(
        kernel,
        tenants,
        n // step,
        [low, block, block, block, table_spec(m, ff, at_rd)],
        (block, block),
        (jax.ShapeDtypeStruct((n, ff), BF), jax.ShapeDtypeStruct((n, ff), BF)),
        [(step, ff)],
        cost(2 * n * step * ff, 2 * (5 * n + m) * ff, n * ff),
        [grad_low, gate_pre, up_pre, base, table],
    )


def low_backs(tenants, gate_grad, up_grad, table, rank, step=256):
    n, ff = gate_grad.shape
    m = table.shape[0]

    def kernel(k_ref, g_ref, u_ref, t_ref, o_ref, held):
        own_factors(k_ref, t_ref, held, rank)
        o_ref[:rank, :] = pick(dot(held[:, :ff], g_ref[...], NT), rank)
        o_ref[rank:, :] = pick(dot(held[:, ff:], u_ref[...], NT), rank)

    block = pl.BlockSpec((step, ff), lambda i, k: (i, 0))
    return call(
        kernel,
        tenants,
        n // step,
        [block, block, table_spec(m, 2 * ff, 0)],
        pl.BlockSpec((2 * rank, step), lambda i, k: (0, i)),
        jax.ShapeDtypeStruct((2 * rank, n), BF),
        [(step, 2 * ff)],
        cost(4 * n * step * ff, 4 * (n + m) * ff),
        [gate_grad, up_grad, table],
    )


def input_part(tenants, backs, table, at_rg, d, step=256):
    rank, n = backs.shape[0] // 2, backs.shape[1]
    m = table.shape[0]

    def kernel(k_ref, l_ref, t_ref, o_ref, held):
        own_factors(k_ref, t_ref, held, rank)
        total = dot(widen(l_ref[:rank, :]), held[:, :d], NN)
        total = total + dot(widen(l_ref[rank:, :]), held[:, d:], NN)
        o_ref[...] = total.astype(BF)

    return call(
        kernel,
        tenants,
        n // step,
        [pl.BlockSpec((2 * rank, step), lambda i, k: (0, i)), table_spec(m, 2 * d, at_rg)],
        pl.BlockSpec((step, d), lambda i, k: (i, 0)),
        jax.ShapeDtypeStruct((n, d), BF),
        [(step, 2 * d)],
        cost(4 * n * step * d, 2 * (n + 2 * m) * d),
        [backs, table],
    )


def outer(lows, rows, row_ids, col_ids, total, at=0, into=None, step=256):
    rank, n = lows[0].shape
    m = col_ids.shape[0]
    k = len(rows)
    widths = [r[0].shape[-1] if isinstance(r, tuple) else r.shape[1] for r in rows]
    width = sum(widths)

    def kernel(row_ref, col_ref, *refs):
        same = col_ref[...] == row_ref[...]
        done = 0
        for low_ref, y_ref, size in zip(refs[:k], refs[k : 2 * k], widths):
            part = dot(widen_t(low_ref[...], same), flat(y_ref), NN)
            refs[-1][:, done : done + size] = part.astype(BF)
            done += size

    specs = [pl.BlockSpec((1, n), lambda i: (0, 0)), pl.BlockSpec((step, 1), lambda i: (i, 0))]
    specs += [pl.BlockSpec((rank, n), lambda i: (0, 0)) for _ in lows]
    specs += [
        fixed_rows(*r) if isinstance(r, tuple) else pl.BlockSpec(r.shape, lambda i: (0, 0))
        for r in rows
    ]
    operands = [row_ids, col_ids, *lows, *[r[0] if isinstance(r, tuple) else r for r in rows]]
    aliases = {}
    if into is not None:
        aliases = {len(operands): 0}
        specs.append(pl.BlockSpec(memory_space=pl.ANY))
        operands.append(into)
    if width == total:
        out_spec = pl.BlockSpec((step, total), lambda i: (i, 0))
    else:
        out_spec = pl.BlockSpec((pl.Element(step), pl.Element(width)), lambda i: (i * step, at))
    return pl.pallas_call(
        kernel,
        grid=(m // step,),
        in_specs=specs,
        out_specs=out_spec,
        out_shape=jax.ShapeDtypeStruct((m, total), BF),
        input_output_aliases=aliases,
        compiler_params=PARAMS,
        cost_estimate=cost(2 * n * m * width, 2 * (n + m) * width),
    )(*operands)


def ring_pairs(chips):
    n_dp = 2 * chips
    return (
        [(i, i ^ 1) for i in range(n_dp)],
        [(i, (i + 2) % n_dp) for i in range(n_dp)],
        [(i, (i - 2) % n_dp) for i in range(n_dp)],
    )


def ring_scatter(parts, chips):
    swap, up, down = ring_pairs(chips)
    half = chips // 2
    theirs = lax.ppermute(parts[0], "dp", swap)
    both = lambda j: parts[1][j].astype(F32) + theirs[j].astype(F32)
    rising = both(half).astype(BF)
    falling = both(half + 1).astype(BF) if half + 1 < chips else None
    for step in range(1, half + 1):
        arrived = lax.ppermute(rising, "dp", up)
        j = half - step
        if j > 0:
            rising = (arrived.astype(F32) + both(j)).astype(BF)
        else:
            last_up = arrived
        if step < half:
            arrived = lax.ppermute(falling, "dp", down)
            j = half + 1 + step
            if j < chips:
                falling = (arrived.astype(F32) + both(j)).astype(BF)
            else:
                last_down = arrived
    return last_up.astype(F32) + last_down.astype(F32) + both(0)


def local(
    inputs,
    grad_out,
    gate_pre,
    up_pre,
    hidden_base,
    block_tenant,
    reduce_gate,
    expand_gate,
    reduce_up,
    expand_up,
    reduce_down,
    expand_down,
):
    n_dp = lax.axis_size("dp")
    chips = n_dp // 2
    own, rank, ff = expand_gate.shape
    d = expand_down.shape[2]
    m = own * n_dp * rank
    n = gate_pre.shape[0]
    flip = lambda t: jnp.swapaxes(t, 1, 2)
    packed, expands = pack(
        [
            [expand_down, flip(reduce_gate), flip(reduce_up), flip(reduce_down)],
            [expand_gate, expand_up],
        ]
    )
    at_ed, at_rg, at_rd = 0, d, 3 * d
    table = lax.all_gather(packed, "dp", axis=0, tiled=True)
    expand = lax.all_gather(expands, "dp", axis=0, tiled=True)

    row_ids = jnp.repeat(block_tenant, n // block_tenant.shape[0])[None, :]
    spot = jnp.arange(m, dtype=jnp.int32)
    col_ids = (spot // rank)[:, None]
    me = lax.axis_index("dp")
    per = own * rank
    to_core = jnp.where(spot < chips * per, 1 - me % 2, me % 2)
    to_chip = (me // 2 + spot // per) % chips
    far_ids = (own * (2 * to_chip + to_core) + (spot % per) // rank)[:, None]
    peers = lax.axis_size("tensor")

    def exchange(rows):
        split = rows.reshape(rows.shape[0], peers, 1, d).transpose(1, 2, 0, 3)
        return lax.all_to_all(split, "tensor", split_axis=0, concat_axis=0)

    outg = exchange(grad_out)
    inp = exchange(inputs)

    grad_low = plane_sum(low_one(block_tenant, outg, 0, table, at_ed, rank))
    lows, hidden = low_three(
        block_tenant, inp, 0, gate_pre, up_pre, table, at_rg, at_rd, rank
    )
    gate_low, up_low, down_low = jnp.split(plane_sum(lows), 3)
    gate_grad, up_grad = middle(
        block_tenant, grad_low, gate_pre, up_pre, hidden_base, table, at_rd
    )
    backs = low_backs(block_tenant, gate_grad, up_grad, expand, rank)
    down_low, backs = lax.optimization_barrier((down_low, backs))
    early = outer(
        [down_low, grad_low], [(outg, 0), hidden], row_ids, col_ids, d + 3 * ff
    )
    backs = side_sum(backs, "x")
    gate_low, up_low, backs = lax.optimization_barrier((gate_low, up_low, backs))
    early = outer(
        [gate_low, up_low], [gate_grad, up_grad], row_ids, col_ids, d + 3 * ff, d + ff, early
    )
    sums = lax.psum_scatter(early, "dp", scatter_dimension=0, tiled=True).reshape(own, rank, -1)
    backs = side_sum(backs, "y")
    late = outer(
        [backs[:rank], backs[rank:]], [(inp, 0), (inp, 0)], row_ids, far_ids, 2 * d
    )
    dx = input_part(block_tenant, backs, table, at_rg, d)
    input_grad = lax.all_to_all(dx, "tensor", split_axis=0, concat_axis=1, tiled=True)
    last = ring_scatter(late.reshape(2, chips, per, 2 * d), chips).astype(BF)
    last = last.reshape(own, rank, 2 * d)
    return (
        input_grad,
        flip(last[:, :, :d]),
        sums[:, :, d + ff : d + 2 * ff],
        flip(last[:, :, d:]),
        sums[:, :, d + 2 * ff :],
        flip(sums[:, :, d : d + ff]),
        sums[:, :, :d],
    )


def solution(mesh):
    in_specs = (
        P(("dp", "tensor"), None),
        P(("dp", "tensor"), None),
        P("dp", "tensor"),
        P("dp", "tensor"),
        P("dp", "tensor"),
        P("dp"),
        P("dp", "tensor", None),
        P("dp", None, "tensor"),
        P("dp", "tensor", None),
        P("dp", None, "tensor"),
        P("dp", "tensor", None),
        P("dp", None, "tensor"),
    )
    out_specs = (
        P(("dp", "tensor"), None),
        P("dp", "tensor", None),
        P("dp", None, "tensor"),
        P("dp", "tensor", None),
        P("dp", None, "tensor"),
        P("dp", "tensor", None),
        P("dp", None, "tensor"),
    )
    return jax.shard_map(local, mesh=mesh, in_specs=in_specs, out_specs=out_specs, check_vma=False)
```

```python
import jax
import jax.numpy as jnp
from jax import lax
from jax.experimental import pallas as pl
from jax.experimental.pallas import tpu as pltpu
from jax.sharding import Mesh
from jax.sharding import PartitionSpec as P

BF = jnp.bfloat16
F32 = jnp.float32
SIDE = 4
DP = ("z", "core")
NT = (((1,), (1,)), ((), ()))
NN = (((1,), (0,)), ((), ()))
PARAMS = pltpu.CompilerParams(vmem_limit_bytes=56 * 1024 * 1024)


def shift(value, side, step):
    pairs = []
    for y in range(SIDE):
        for x in range(SIDE):
            to_y, to_x = (y, (x + step) % SIDE) if side == "x" else ((y + step) % SIDE, x)
            pairs.append((y * SIDE + x, to_y * SIDE + to_x))
    return lax.ppermute(value, "tensor", pairs)


def side_sum(value, side, beside):
    others = [shift(value, side, step) for step in (1, 3, 2)]
    others, beside = lax.optimization_barrier((others, beside))
    total = value.astype(F32)
    for other in others:
        total = total + other.astype(F32)
    return total.astype(BF), beside


def dot(left, right, dims):
    return lax.dot_general(left, right, dims, preferred_element_type=F32)


def diagonal(size, rank):
    down = lax.broadcasted_iota(jnp.int32, (size, size), 0) // rank
    across = lax.broadcasted_iota(jnp.int32, (size, size), 1) // rank
    return down == across


def own_factors(tenant_ref, table_ref, held, rank):
    count = held.shape[0] // rank
    first = pl.program_id(0) * count
    for b in range(count):
        at = pl.multiple_of(tenant_ref[first + b] * rank, rank)
        held[b * rank : (b + 1) * rank, :] = table_ref[pl.ds(at, rank), :]


def pick(dense, rank):
    kept = jnp.where(diagonal(dense.shape[0], rank), dense, 0.0)
    return kept.reshape(-1, rank, kept.shape[1]).sum(axis=0).astype(BF)


def widen(low_t):
    rank, step = low_t.shape
    quad = jnp.concatenate([low_t.astype(F32)] * (128 // rank), axis=0).T
    wide = jnp.concatenate([quad] * (step // 128), axis=1)
    return jnp.where(diagonal(step, rank), wide, 0.0).astype(BF)


def widen_t(low_t, same):
    wide = jnp.concatenate([low_t.astype(F32)] * (same.shape[0] // low_t.shape[0]), axis=0)
    return jnp.where(same, wide, 0.0).astype(BF)


def table_spec(m, width, at):
    return pl.BlockSpec((pl.Element(m), pl.Element(width)), lambda i, k: (0, at))


def cost(flops, moved, exps=0):
    return pl.CostEstimate(flops=flops, bytes_accessed=moved, transcendentals=exps)


def pack(groups):
    own, rank, _ = groups[0][0].shape
    flat = [part for group in groups for part in group]

    def kernel(*refs):
        ins, outs = list(refs[: len(flat)]), refs[len(flat) :]
        for out, group in zip(outs, groups):
            at = 0
            for part in group:
                ref = ins.pop(0)
                for t in range(own):
                    out[t * rank : (t + 1) * rank, at : at + part.shape[2]] = ref[t]
                at += part.shape[2]

    shapes = [
        jax.ShapeDtypeStruct((own * rank, sum(part.shape[2] for part in group)), BF)
        for group in groups
    ]
    return pl.pallas_call(kernel, out_shape=shapes, compiler_params=PARAMS)(*flat)


def rows_spec(swapped, which, step):
    _, _, each, width = swapped.shape
    return pl.BlockSpec((step // each, 1, each, width), lambda i, k: (i, which, 0, 0))


def flat(ref):
    return ref[...].reshape(-1, ref.shape[-1])


def call(kernel, tenants, grid, in_specs, out_specs, out_shape, held, estimate, operands):
    return pl.pallas_call(
        kernel,
        grid_spec=pltpu.PrefetchScalarGridSpec(
            num_scalar_prefetch=1,
            grid=(grid,),
            in_specs=in_specs,
            out_specs=out_specs,
            scratch_shapes=[pltpu.VMEM(shape, BF) for shape in held],
        ),
        out_shape=out_shape,
        compiler_params=PARAMS,
        cost_estimate=estimate,
    )(tenants, *operands)


def low_one(tenants, swapped, which, table, at, rank, step=512):
    peers, _, each, width = swapped.shape
    n = peers * each
    m = table.shape[0]

    def kernel(k_ref, a_ref, t_ref, o_ref, held):
        own_factors(k_ref, t_ref, held, rank)
        o_ref[...] = pick(dot(held[...], flat(a_ref), NT), rank)

    return call(
        kernel,
        tenants,
        n // step,
        [rows_spec(swapped, which, step), table_spec(m, width, at)],
        pl.BlockSpec((rank, step), lambda i, k: (0, i)),
        jax.ShapeDtypeStruct((rank, n), BF),
        [(step, width)],
        cost(2 * n * step * width, 2 * (n + m) * width),
        [swapped, table],
    )


def low_three(tenants, swapped, which, gate_pre, up_pre, table, at_rg, at_rd, rank, step=256):
    d = swapped.shape[3]
    n, ff = gate_pre.shape
    m = table.shape[0]

    def kernel(k_ref, x_ref, g_ref, u_ref, rgu_ref, rd_ref, o_ref, h_ref, held, held_rd):
        own_factors(k_ref, rgu_ref, held, rank)
        own_factors(k_ref, rd_ref, held_rd, rank)
        gate = g_ref[...].astype(F32)
        hidden = (gate * jax.nn.sigmoid(gate) * u_ref[...].astype(F32)).astype(BF)
        h_ref[...] = hidden
        rows = flat(x_ref)
        o_ref[:rank, :] = pick(dot(held[:, :d], rows, NT), rank)
        o_ref[rank : 2 * rank, :] = pick(dot(held[:, d:], rows, NT), rank)
        o_ref[2 * rank :, :] = pick(dot(held_rd[...], hidden, NT), rank)

    block = pl.BlockSpec((step, ff), lambda i, k: (i, 0))
    return call(
        kernel,
        tenants,
        n // step,
        [
            rows_spec(swapped, which, step),
            block,
            block,
            table_spec(m, 2 * d, at_rg),
            table_spec(m, ff, at_rd),
        ],
        (pl.BlockSpec((3 * rank, step), lambda i, k: (0, i)), block),
        (jax.ShapeDtypeStruct((3 * rank, n), BF), jax.ShapeDtypeStruct((n, ff), BF)),
        [(step, 2 * d), (step, ff)],
        cost(2 * n * step * (2 * d + ff), 2 * (n + 2 * m) * d + 2 * (3 * n + m) * ff, n * ff),
        [swapped, gate_pre, up_pre, table, table],
    )


def middle(tenants, grad_low, gate_pre, up_pre, base, table, at_rd, step=256):
    n, ff = gate_pre.shape
    rank = grad_low.shape[0]
    m = table.shape[0]

    def kernel(k_ref, l_ref, g_ref, u_ref, b_ref, rd_ref, gg_ref, ug_ref, held):
        own_factors(k_ref, rd_ref, held, rank)
        grad = b_ref[...].astype(F32) + dot(widen(l_ref[...]), held[...], NN)
        gate = g_ref[...].astype(F32)
        s = jax.nn.sigmoid(gate)
        slope = s * (1.0 + gate * (1.0 - s))
        gg_ref[...] = (grad * u_ref[...].astype(F32) * slope).astype(BF)
        ug_ref[...] = (grad * (gate * s)).astype(BF)

    block = pl.BlockSpec((step, ff), lambda i, k: (i, 0))
    low = pl.BlockSpec((rank, step), lambda i, k: (0, i))
    return call(
        kernel,
        tenants,
        n // step,
        [low, block, block, block, table_spec(m, ff, at_rd)],
        (block, block),
        (jax.ShapeDtypeStruct((n, ff), BF), jax.ShapeDtypeStruct((n, ff), BF)),
        [(step, ff)],
        cost(2 * n * step * ff, 2 * (5 * n + m) * ff, n * ff),
        [grad_low, gate_pre, up_pre, base, table],
    )


def low_backs(tenants, gate_grad, up_grad, table, rank, step=256):
    n, ff = gate_grad.shape
    m = table.shape[0]

    def kernel(k_ref, g_ref, u_ref, t_ref, o_ref, held):
        own_factors(k_ref, t_ref, held, rank)
        o_ref[:rank, :] = pick(dot(held[:, :ff], g_ref[...], NT), rank)
        o_ref[rank:, :] = pick(dot(held[:, ff:], u_ref[...], NT), rank)

    block = pl.BlockSpec((step, ff), lambda i, k: (i, 0))
    return call(
        kernel,
        tenants,
        n // step,
        [block, block, table_spec(m, 2 * ff, 0)],
        pl.BlockSpec((2 * rank, step), lambda i, k: (0, i)),
        jax.ShapeDtypeStruct((2 * rank, n), BF),
        [(step, 2 * ff)],
        cost(4 * n * step * ff, 4 * (n + m) * ff),
        [gate_grad, up_grad, table],
    )


def input_part(tenants, backs, table, at_rg, d, step=256):
    rank, n = backs.shape[0] // 2, backs.shape[1]
    m = table.shape[0]

    def kernel(k_ref, l_ref, t_ref, o_ref, held):
        own_factors(k_ref, t_ref, held, rank)
        total = dot(widen(l_ref[:rank, :]), held[:, :d], NN)
        total = total + dot(widen(l_ref[rank:, :]), held[:, d:], NN)
        o_ref[...] = total.astype(BF)

    return call(
        kernel,
        tenants,
        n // step,
        [pl.BlockSpec((2 * rank, step), lambda i, k: (0, i)), table_spec(m, 2 * d, at_rg)],
        pl.BlockSpec((step, d), lambda i, k: (i, 0)),
        jax.ShapeDtypeStruct((n, d), BF),
        [(step, 2 * d)],
        cost(4 * n * step * d, 2 * (n + 2 * m) * d),
        [backs, table],
    )


def outer(lows, rows, row_ids, place, turned, other, chips, own, plus=None, step=256):
    rank, n = lows[0].shape
    per = own * rank
    m = chips * per
    k = len(lows)
    widths = [r.shape[-1] for r in rows]
    starts = [sum(widths[:j]) for j in range(k)]
    total = sum(widths)
    sources = []
    for r in rows:
        if not any(r is known for known in sources):
            sources.append(r)
    source_of = [[r is known for known in sources].index(True) for r in rows]
    loads = sources + ([] if plus is None else [plus])
    count = len(loads)

    def kernel(place_ref, row_ref, *refs):
        low_refs, refs = refs[:k], refs[k:]
        load_refs, out_ref = refs[:count], refs[count]
        buffers, made, in_sem, out_sem = refs[count + 1 : -3], refs[-3], refs[-2], refs[-1]
        copies = [
            pltpu.make_async_copy(ref, buffer, in_sem.at[j])
            for j, (ref, buffer) in enumerate(zip(load_refs, buffers))
        ]
        started = set()
        for j in range(k):
            if source_of[j] not in started:
                copies[source_of[j]].start()
                started.add(source_of[j])
        row = row_ref[...]
        from_chip = place_ref[0] if turned else 0
        at_core = 1 - place_ref[1] if other else place_ref[1]
        results = []
        for j, (at, size) in enumerate(zip(starts, widths)):
            low = low_refs[j][...]
            if source_of[j] in started:
                copies[source_of[j]].wait()
                started.remove(source_of[j])
            for i in range(0, m, step):
                spot = i + lax.broadcasted_iota(jnp.int32, (step, 1), 0)
                chip = (from_chip + spot // per) % chips
                tenant = own * (2 * chip + at_core) + (spot % per) // rank
                part = dot(widen_t(low, tenant == row), flat(buffers[source_of[j]]), NN)
                if plus is not None:
                    part = part + load_refs[-1][i : i + step, at : at + size].astype(F32)
                made[i : i + step, at : at + size] = part.astype(BF)

            result = pltpu.make_async_copy(
                made.at[:, at : at + size], out_ref.at[:, at : at + size], out_sem.at[j]
            )
            result.start()
            results.append(result)
        for result in results:
            result.wait()

    anywhere = pl.BlockSpec(memory_space=pl.ANY)
    return pl.pallas_call(
        kernel,
        in_specs=[
            pl.BlockSpec(memory_space=pltpu.SMEM),
            *[pl.BlockSpec(memory_space=pltpu.VMEM)] * (1 + k),
            *[anywhere] * len(sources),
            *[pl.BlockSpec(memory_space=pltpu.VMEM)] * (count - len(sources)),
        ],
        out_specs=anywhere,
        out_shape=jax.ShapeDtypeStruct((m, total), BF),
        scratch_shapes=[
            *[pltpu.VMEM(array.shape, BF) for array in sources],
            pltpu.VMEM((m, total), BF),
            pltpu.SemaphoreType.DMA((len(sources),)),
            pltpu.SemaphoreType.DMA((k,)),
        ],
        compiler_params=PARAMS,
        cost_estimate=cost(2 * n * m * total, 2 * (n + m) * total),
    )(place, row_ids, *lows, *loads)


def ring_pairs(chips):
    n_dp = 2 * chips
    return (
        [(i, i ^ 1) for i in range(n_dp)],
        [(i, (i + 2) % n_dp) for i in range(n_dp)],
        [(i, (i - 2) % n_dp) for i in range(n_dp)],
    )


def to_other_core(value, chips):
    return lax.ppermute(value, DP, ring_pairs(chips)[0])


def ring_scatter(theirs, mine, chips, beside, finished):
    _, up, down = ring_pairs(chips)
    half = chips // 2
    both = lambda j: mine[j].astype(F32) + theirs[j].astype(F32)
    rising = both(half).astype(BF)
    falling = both(half + 1).astype(BF)
    for step in range(1, half + 1):
        risen = lax.ppermute(rising, DP, up)
        if step < half:
            fallen = lax.ppermute(falling, DP, down)
        if step == 1:
            risen, fallen, _ = lax.optimization_barrier((risen, fallen, beside))
        if step < half:
            rising = (risen.astype(F32) + both(half - step)).astype(BF)
        if step < half - 1:
            falling = (fallen.astype(F32) + both(half + 1 + step)).astype(BF)
    risen, finished = lax.optimization_barrier((risen, finished))
    return risen.astype(F32) + fallen.astype(F32) + both(0), finished


def local(
    inputs,
    grad_out,
    gate_pre,
    up_pre,
    hidden_base,
    block_tenant,
    reduce_gate,
    expand_gate,
    reduce_up,
    expand_up,
    reduce_down,
    expand_down,
):
    chips = lax.axis_size("z")
    n_dp = 2 * chips
    own, rank, ff = expand_gate.shape
    d = expand_down.shape[2]
    m = own * n_dp * rank
    n = gate_pre.shape[0]
    flip = lambda t: jnp.swapaxes(t, 1, 2)
    packed, expands = pack(
        [
            [expand_down, flip(reduce_gate), flip(reduce_up), flip(reduce_down)],
            [expand_gate, expand_up],
        ]
    )
    at_ed, at_rg, at_rd = 0, d, 3 * d
    table = lax.all_gather(packed, DP, axis=0, tiled=True)
    expand = lax.all_gather(expands, DP, axis=0, tiled=True)

    row_ids = jnp.repeat(block_tenant, n // block_tenant.shape[0])[None, :]
    per = own * rank
    place = jnp.stack([lax.axis_index("z"), lax.axis_index("core")]).astype(jnp.int32)
    peers = lax.axis_size("tensor")

    def exchange(rows):
        split = rows.reshape(rows.shape[0], peers, 1, d).transpose(1, 2, 0, 3)
        return lax.all_to_all(split, "tensor", split_axis=0, concat_axis=0)

    outg = exchange(grad_out)
    inp = exchange(inputs)

    grad_low = low_one(block_tenant, outg, 0, table, at_ed, rank)
    grad_low, _ = side_sum(grad_low, "x", ())
    low_made = low_three(block_tenant, inp, 0, gate_pre, up_pre, table, at_rg, at_rd, rank)
    grad_low, (lows, hidden) = side_sum(grad_low, "y", low_made)
    grads = middle(block_tenant, grad_low, gate_pre, up_pre, hidden_base, table, at_rd)
    lows, (gate_grad, up_grad) = side_sum(lows, "x", grads)
    backs = low_backs(block_tenant, gate_grad, up_grad, expand, rank)
    lows, backs = side_sum(lows, "y", backs)
    gate_low, up_low, down_low = jnp.split(lows, 3)
    early = (
        [down_low, grad_low, gate_low, up_low],
        [outg, hidden, gate_grad, up_grad],
        row_ids,
        place,
        False,
    )
    theirs = outer(*early, True, chips, own)
    backs, theirs = side_sum(backs, "x", theirs)
    theirs = to_other_core(theirs, chips)
    mine = outer(*early, False, chips, own, theirs)
    backs, mine = side_sum(backs, "y", mine)
    sums = lax.psum_scatter(mine, "z", scatter_dimension=0, tiled=True).reshape(own, rank, -1)
    late = ([backs[:rank], backs[rank:]], [inp, inp], row_ids, place, True)
    by_chip = lambda a: a.reshape(chips, per, 2 * d)
    theirs = to_other_core(by_chip(outer(*late, True, chips, own)), chips)
    mine = by_chip(outer(*late, False, chips, own))
    dx = input_part(block_tenant, backs, table, at_rg, d)
    done = (
        sums[:, :, :d],
        flip(sums[:, :, d : d + ff]),
        sums[:, :, d + ff : d + 2 * ff],
        sums[:, :, d + 2 * ff :],
    )
    last, done = ring_scatter(theirs, mine, chips, dx, done)
    sum_ed, sum_rd, sum_eg, sum_eu = done
    input_grad = lax.all_to_all(dx, "tensor", split_axis=0, concat_axis=1, tiled=True)
    last = last.astype(BF).reshape(own, rank, 2 * d)
    return (
        input_grad,
        flip(last[:, :, :d]),
        sum_eg,
        flip(last[:, :, d:]),
        sum_eu,
        sum_rd,
        sum_ed,
    )


def solution(mesh):
    grid = mesh.devices
    mesh = Mesh(grid.reshape(-1, 2, grid.shape[1]), (*DP, "tensor"))
    in_specs = (
        P((*DP, "tensor"), None),
        P((*DP, "tensor"), None),
        P(DP, "tensor"),
        P(DP, "tensor"),
        P(DP, "tensor"),
        P(DP),
        P(DP, "tensor", None),
        P(DP, None, "tensor"),
        P(DP, "tensor", None),
        P(DP, None, "tensor"),
        P(DP, "tensor", None),
        P(DP, None, "tensor"),
    )
    out_specs = (
        P((*DP, "tensor"), None),
        P(DP, "tensor", None),
        P(DP, None, "tensor"),
        P(DP, "tensor", None),
        P(DP, None, "tensor"),
        P(DP, "tensor", None),
        P(DP, None, "tensor"),
    )
    return jax.shard_map(local, mesh=mesh, in_specs=in_specs, out_specs=out_specs, check_vma=False)
```

```python
import jax
import jax.numpy as jnp
from jax import lax
from jax.experimental import pallas as pl
from jax.experimental.pallas import tpu as pltpu
from jax.sharding import Mesh
from jax.sharding import PartitionSpec as P

BF = jnp.bfloat16
F32 = jnp.float32
SIDE = 4
DP = ("z", "core")
NT = (((1,), (1,)), ((), ()))
NN = (((1,), (0,)), ((), ()))
PARAMS = pltpu.CompilerParams(vmem_limit_bytes=56 * 1024 * 1024)


def shift(value, side, step):
    pairs = []
    for y in range(SIDE):
        for x in range(SIDE):
            to_y, to_x = (y, (x + step) % SIDE) if side == "x" else ((y + step) % SIDE, x)
            pairs.append((y * SIDE + x, to_y * SIDE + to_x))
    return lax.ppermute(value, "tensor", pairs)


def side_sum(value, side, beside):
    others = [shift(value, side, step) for step in (1, 3, 2)]
    others, beside = lax.optimization_barrier((others, beside))
    total = value.astype(F32)
    for other in others:
        total = total + other.astype(F32)
    return total.astype(BF), beside


def dot(left, right, dims):
    return lax.dot_general(left, right, dims, preferred_element_type=F32)


def diagonal(size, rank):
    down = lax.broadcasted_iota(jnp.int32, (size, size), 0) // rank
    across = lax.broadcasted_iota(jnp.int32, (size, size), 1) // rank
    return down == across


def own_factors(tenant_ref, table_ref, held, rank):
    count = held.shape[0] // rank
    first = pl.program_id(0) * count
    for b in range(count):
        at = pl.multiple_of(tenant_ref[first + b] * rank, rank)
        held[b * rank : (b + 1) * rank, :] = table_ref[pl.ds(at, rank), :]


def pick(dense, rank):
    kept = jnp.where(diagonal(dense.shape[0], rank), dense, 0.0)
    return kept.reshape(-1, rank, kept.shape[1]).sum(axis=0).astype(BF)


def widen(low_t):
    rank, step = low_t.shape
    quad = jnp.concatenate([low_t.astype(F32)] * (128 // rank), axis=0).T
    wide = jnp.concatenate([quad] * (step // 128), axis=1)
    return jnp.where(diagonal(step, rank), wide, 0.0).astype(BF)


def widen_t(low_t, same):
    wide = jnp.concatenate([low_t.astype(F32)] * (same.shape[0] // low_t.shape[0]), axis=0)
    return jnp.where(same, wide, 0.0).astype(BF)


def table_spec(m, width, at):
    return pl.BlockSpec((pl.Element(m), pl.Element(width)), lambda i, k: (0, at))


def cost(flops, moved, exps=0):
    return pl.CostEstimate(flops=flops, bytes_accessed=moved, transcendentals=exps)


def pack(groups):
    own, rank, _ = groups[0][0].shape
    flat = [part for group in groups for part in group]

    def kernel(*refs):
        ins, outs = list(refs[: len(flat)]), refs[len(flat) :]
        for out, group in zip(outs, groups):
            at = 0
            for part in group:
                ref = ins.pop(0)
                for t in range(own):
                    out[t * rank : (t + 1) * rank, at : at + part.shape[2]] = ref[t]
                at += part.shape[2]

    shapes = [
        jax.ShapeDtypeStruct((own * rank, sum(part.shape[2] for part in group)), BF)
        for group in groups
    ]
    return pl.pallas_call(kernel, out_shape=shapes, compiler_params=PARAMS)(*flat)


def rows_spec(swapped, which, step):
    _, _, each, width = swapped.shape
    return pl.BlockSpec((step // each, 1, each, width), lambda i, k: (i, which, 0, 0))


def flat(ref):
    return ref[...].reshape(-1, ref.shape[-1])


def call(kernel, tenants, grid, in_specs, out_specs, out_shape, held, estimate, operands):
    return pl.pallas_call(
        kernel,
        grid_spec=pltpu.PrefetchScalarGridSpec(
            num_scalar_prefetch=1,
            grid=(grid,),
            in_specs=in_specs,
            out_specs=out_specs,
            scratch_shapes=[pltpu.VMEM(shape, BF) for shape in held],
        ),
        out_shape=out_shape,
        compiler_params=PARAMS,
        cost_estimate=estimate,
    )(tenants, *operands)


def low_one(tenants, swapped, which, table, at, rank, step=512):
    peers, _, each, width = swapped.shape
    n = peers * each
    m = table.shape[0]

    def kernel(k_ref, a_ref, t_ref, o_ref, held):
        own_factors(k_ref, t_ref, held, rank)
        o_ref[...] = pick(dot(held[...], flat(a_ref), NT), rank)

    return call(
        kernel,
        tenants,
        n // step,
        [rows_spec(swapped, which, step), table_spec(m, width, at)],
        pl.BlockSpec((rank, step), lambda i, k: (0, i)),
        jax.ShapeDtypeStruct((rank, n), BF),
        [(step, width)],
        cost(2 * n * step * width, 2 * (n + m) * width),
        [swapped, table],
    )


def low_three(tenants, swapped, which, gate_pre, up_pre, table, at_rg, at_rd, rank, step=256):
    d = swapped.shape[3]
    n, ff = gate_pre.shape
    m = table.shape[0]

    def kernel(k_ref, x_ref, g_ref, u_ref, rgu_ref, rd_ref, o_ref, h_ref, held, held_rd):
        own_factors(k_ref, rgu_ref, held, rank)
        own_factors(k_ref, rd_ref, held_rd, rank)
        gate = g_ref[...].astype(F32)
        hidden = (gate * jax.nn.sigmoid(gate) * u_ref[...].astype(F32)).astype(BF)
        h_ref[...] = hidden
        rows = flat(x_ref)
        o_ref[:rank, :] = pick(dot(held[:, :d], rows, NT), rank)
        o_ref[rank : 2 * rank, :] = pick(dot(held[:, d:], rows, NT), rank)
        o_ref[2 * rank :, :] = pick(dot(held_rd[...], hidden, NT), rank)

    block = pl.BlockSpec((step, ff), lambda i, k: (i, 0))
    return call(
        kernel,
        tenants,
        n // step,
        [
            rows_spec(swapped, which, step),
            block,
            block,
            table_spec(m, 2 * d, at_rg),
            table_spec(m, ff, at_rd),
        ],
        (pl.BlockSpec((3 * rank, step), lambda i, k: (0, i)), block),
        (jax.ShapeDtypeStruct((3 * rank, n), BF), jax.ShapeDtypeStruct((n, ff), BF)),
        [(step, 2 * d), (step, ff)],
        cost(2 * n * step * (2 * d + ff), 2 * (n + 2 * m) * d + 2 * (3 * n + m) * ff, n * ff),
        [swapped, gate_pre, up_pre, table, table],
    )


def middle(tenants, grad_low, gate_pre, up_pre, base, table, at_rd, step=256):
    n, ff = gate_pre.shape
    rank = grad_low.shape[0]
    m = table.shape[0]

    def kernel(k_ref, l_ref, g_ref, u_ref, b_ref, rd_ref, gg_ref, ug_ref, held):
        own_factors(k_ref, rd_ref, held, rank)
        grad = b_ref[...].astype(F32) + dot(widen(l_ref[...]), held[...], NN)
        gate = g_ref[...].astype(F32)
        s = jax.nn.sigmoid(gate)
        slope = s * (1.0 + gate * (1.0 - s))
        gg_ref[...] = (grad * u_ref[...].astype(F32) * slope).astype(BF)
        ug_ref[...] = (grad * (gate * s)).astype(BF)

    block = pl.BlockSpec((step, ff), lambda i, k: (i, 0))
    low = pl.BlockSpec((rank, step), lambda i, k: (0, i))
    return call(
        kernel,
        tenants,
        n // step,
        [low, block, block, block, table_spec(m, ff, at_rd)],
        (block, block),
        (jax.ShapeDtypeStruct((n, ff), BF), jax.ShapeDtypeStruct((n, ff), BF)),
        [(step, ff)],
        cost(2 * n * step * ff, 2 * (5 * n + m) * ff, n * ff),
        [grad_low, gate_pre, up_pre, base, table],
    )


def low_backs(tenants, gate_grad, up_grad, table, rank, step=256):
    n, ff = gate_grad.shape
    m = table.shape[0]

    def kernel(k_ref, g_ref, u_ref, t_ref, o_ref, held):
        own_factors(k_ref, t_ref, held, rank)
        o_ref[:rank, :] = pick(dot(held[:, :ff], g_ref[...], NT), rank)
        o_ref[rank:, :] = pick(dot(held[:, ff:], u_ref[...], NT), rank)

    block = pl.BlockSpec((step, ff), lambda i, k: (i, 0))
    return call(
        kernel,
        tenants,
        n // step,
        [block, block, table_spec(m, 2 * ff, 0)],
        pl.BlockSpec((2 * rank, step), lambda i, k: (0, i)),
        jax.ShapeDtypeStruct((2 * rank, n), BF),
        [(step, 2 * ff)],
        cost(4 * n * step * ff, 4 * (n + m) * ff),
        [gate_grad, up_grad, table],
    )


def input_part(tenants, backs, table, at_rg, d, step=256):
    rank, n = backs.shape[0] // 2, backs.shape[1]
    m = table.shape[0]

    def kernel(k_ref, l_ref, t_ref, o_ref, held):
        own_factors(k_ref, t_ref, held, rank)
        total = dot(widen(l_ref[:rank, :]), held[:, :d], NN)
        total = total + dot(widen(l_ref[rank:, :]), held[:, d:], NN)
        o_ref[...] = total.astype(BF)

    return call(
        kernel,
        tenants,
        n // step,
        [pl.BlockSpec((2 * rank, step), lambda i, k: (0, i)), table_spec(m, 2 * d, at_rg)],
        pl.BlockSpec((step, d), lambda i, k: (i, 0)),
        jax.ShapeDtypeStruct((n, d), BF),
        [(step, 2 * d)],
        cost(4 * n * step * d, 2 * (n + 2 * m) * d),
        [backs, table],
    )


def outer(lows, rows, row_ids, place, turned, other, chips, own, plus=None, step=128):
    rank, n = lows[0].shape
    per = own * rank
    m = chips * per
    k = len(lows)
    widths = [r.shape[-1] for r in rows]
    starts = [sum(widths[:j]) for j in range(k)]
    total = sum(widths)
    sources = []
    for r in rows:
        if not any(r is known for known in sources):
            sources.append(r)
    source_of = [[r is known for known in sources].index(True) for r in rows]
    loads = sources + ([] if plus is None else [plus])
    count = len(loads)

    def kernel(place_ref, row_ref, *refs):
        low_refs, load_refs, out_ref = refs[:k], refs[k : k + count], refs[k + count]
        from_chip = place_ref[0] if turned else 0
        at_core = 1 - place_ref[1] if other else place_ref[1]
        spot = pl.program_id(0) * step + lax.broadcasted_iota(jnp.int32, (step, 1), 0)
        chip = (from_chip + spot // per) % chips
        same = own * (2 * chip + at_core) + (spot % per) // rank == row_ref[...]
        for j, (at, size) in enumerate(zip(starts, widths)):
            wide = widen_t(low_refs[j][...], same)
            part = dot(wide, flat(load_refs[source_of[j]]), NN)
            if plus is not None:
                part = part + load_refs[-1][:, at : at + size].astype(F32)
            out_ref[:, at : at + size] = part.astype(BF)

    once = lambda a: pl.BlockSpec(a.shape, lambda i, nd=a.ndim: (0,) * nd)
    block = pl.BlockSpec((step, total), lambda i: (i, 0))
    return pl.pallas_call(
        kernel,
        grid=(m // step,),
        in_specs=[
            pl.BlockSpec(memory_space=pltpu.SMEM),
            *[once(a) for a in (row_ids, *lows, *sources)],
            *[block] * (count - len(sources)),
        ],
        out_specs=block,
        out_shape=jax.ShapeDtypeStruct((m, total), BF),
        compiler_params=PARAMS,
        cost_estimate=cost(2 * n * m * total, 2 * (n + m) * total),
    )(place, row_ids, *lows, *loads)


def ring_pairs(chips):
    n_dp = 2 * chips
    return (
        [(i, i ^ 1) for i in range(n_dp)],
        [(i, (i + 2) % n_dp) for i in range(n_dp)],
        [(i, (i - 2) % n_dp) for i in range(n_dp)],
    )


def to_other_core(value, chips):
    return lax.ppermute(value, DP, ring_pairs(chips)[0])


def ring_scatter(theirs, mine, chips, beside, finished):
    _, up, down = ring_pairs(chips)
    half = chips // 2
    both = lambda j: mine[j].astype(F32) + theirs[j].astype(F32)
    rising = both(half).astype(BF)
    falling = both(half + 1).astype(BF)
    for step in range(1, half + 1):
        risen = lax.ppermute(rising, DP, up)
        if step < half:
            fallen = lax.ppermute(falling, DP, down)
        if step == 1:
            risen, fallen, _ = lax.optimization_barrier((risen, fallen, beside))
        if step < half:
            rising = (risen.astype(F32) + both(half - step)).astype(BF)
        if step < half - 1:
            falling = (fallen.astype(F32) + both(half + 1 + step)).astype(BF)
    risen, finished = lax.optimization_barrier((risen, finished))
    return risen.astype(F32) + fallen.astype(F32) + both(0), finished


def local(
    inputs,
    grad_out,
    gate_pre,
    up_pre,
    hidden_base,
    block_tenant,
    reduce_gate,
    expand_gate,
    reduce_up,
    expand_up,
    reduce_down,
    expand_down,
):
    chips = lax.axis_size("z")
    n_dp = 2 * chips
    own, rank, ff = expand_gate.shape
    d = expand_down.shape[2]
    m = own * n_dp * rank
    n = gate_pre.shape[0]
    flip = lambda t: jnp.swapaxes(t, 1, 2)
    packed, expands = pack(
        [
            [expand_down, flip(reduce_gate), flip(reduce_up), flip(reduce_down)],
            [expand_gate, expand_up],
        ]
    )
    at_ed, at_rg, at_rd = 0, d, 3 * d
    table = lax.all_gather(packed, DP, axis=0, tiled=True)
    expand = lax.all_gather(expands, DP, axis=0, tiled=True)

    row_ids = jnp.repeat(block_tenant, n // block_tenant.shape[0])[None, :]
    per = own * rank
    place = jnp.stack([lax.axis_index("z"), lax.axis_index("core")]).astype(jnp.int32)
    peers = lax.axis_size("tensor")

    def exchange(rows):
        split = rows.reshape(rows.shape[0], peers, 1, d).transpose(1, 2, 0, 3)
        return lax.all_to_all(split, "tensor", split_axis=0, concat_axis=0)

    outg = exchange(grad_out)
    inp = exchange(inputs)

    grad_low = low_one(block_tenant, outg, 0, table, at_ed, rank)
    grad_low, _ = side_sum(grad_low, "x", ())
    low_made = low_three(block_tenant, inp, 0, gate_pre, up_pre, table, at_rg, at_rd, rank)
    grad_low, (lows, hidden) = side_sum(grad_low, "y", low_made)
    grads = middle(block_tenant, grad_low, gate_pre, up_pre, hidden_base, table, at_rd)
    lows, (gate_grad, up_grad) = side_sum(lows, "x", grads)
    backs = low_backs(block_tenant, gate_grad, up_grad, expand, rank)
    lows, backs = side_sum(lows, "y", backs)
    gate_low, up_low, down_low = jnp.split(lows, 3)
    early = (
        [down_low, grad_low, gate_low, up_low],
        [outg, hidden, gate_grad, up_grad],
        row_ids,
        place,
        False,
    )
    theirs = outer(*early, True, chips, own)
    backs, theirs = side_sum(backs, "x", theirs)
    theirs = to_other_core(theirs, chips)
    mine = outer(*early, False, chips, own, theirs)
    backs, mine = side_sum(backs, "y", mine)
    sums = lax.psum_scatter(mine, "z", scatter_dimension=0, tiled=True).reshape(own, rank, -1)
    late = ([backs[:rank], backs[rank:]], [inp, inp], row_ids, place, True)
    by_chip = lambda a: a.reshape(chips, per, 2 * d)
    theirs = to_other_core(by_chip(outer(*late, True, chips, own)), chips)
    mine = by_chip(outer(*late, False, chips, own))
    dx = input_part(block_tenant, backs, table, at_rg, d)
    done = (
        sums[:, :, :d],
        flip(sums[:, :, d : d + ff]),
        sums[:, :, d + ff : d + 2 * ff],
        sums[:, :, d + 2 * ff :],
    )
    last, done = ring_scatter(theirs, mine, chips, dx, done)
    sum_ed, sum_rd, sum_eg, sum_eu = done
    input_grad = lax.all_to_all(dx, "tensor", split_axis=0, concat_axis=1, tiled=True)
    last = last.astype(BF).reshape(own, rank, 2 * d)
    return (
        input_grad,
        flip(last[:, :, :d]),
        sum_eg,
        flip(last[:, :, d:]),
        sum_eu,
        sum_rd,
        sum_ed,
    )


def solution(mesh):
    grid = mesh.devices
    mesh = Mesh(grid.reshape(-1, 2, grid.shape[1]), (*DP, "tensor"))
    in_specs = (
        P((*DP, "tensor"), None),
        P((*DP, "tensor"), None),
        P(DP, "tensor"),
        P(DP, "tensor"),
        P(DP, "tensor"),
        P(DP),
        P(DP, "tensor", None),
        P(DP, None, "tensor"),
        P(DP, "tensor", None),
        P(DP, None, "tensor"),
        P(DP, "tensor", None),
        P(DP, None, "tensor"),
    )
    out_specs = (
        P((*DP, "tensor"), None),
        P(DP, "tensor", None),
        P(DP, None, "tensor"),
        P(DP, "tensor", None),
        P(DP, None, "tensor"),
        P(DP, "tensor", None),
        P(DP, None, "tensor"),
    )
    return jax.shard_map(local, mesh=mesh, in_specs=in_specs, out_specs=out_specs, check_vma=False)
```
